32 devices in a mesh: section: 2 (over x), ctx: 2 (over y), shard: 8 (over z, core).
Axes of the slice: x: 2, y: 2, z: 4, core: 2. Of those that a mesh axis runs over, the one named last changes fastest.
Arguments:
- inputs: bfloat16 [2, 8, 1024, 576], P(None, 'shard', 'ctx'), may hold values from -6 to 6
- cotangent: bfloat16 [2, 8, 1024, 576], P(None, 'shard', 'ctx'), may hold values from -6 to 6
- attn_gain: bfloat16 [2, 576], P('section', 'shard'), may hold values from 0.5 to 1.5
- w_query: bfloat16 [2, 576, 576], P('section', 'shard'), may hold values from -0.25 to 0.25
- w_key: bfloat16 [2, 576, 192], P('section', 'shard'), may hold values from -0.25 to 0.25
- w_value: bfloat16 [2, 576, 192], P('section', 'shard'), may hold values from -0.25 to 0.25
- w_out: bfloat16 [2, 576, 576], P('section', 'shard'), may hold values from -3 to 3
- mlp_gain: bfloat16 [2, 576], P('section', 'shard'), may hold values from 0.5 to 1.5
- w_gate: bfloat16 [2, 576, 1536], P('section', 'shard'), may hold values from -0.25 to 0.25
- w_up: bfloat16 [2, 576, 1536], P('section', 'shard'), may hold values from -0.25 to 0.25
- w_down: bfloat16 [2, 1536, 576], P('section', 'shard'), may hold values from -0.15625 to 0.15625
Outputs:
- activations: bfloat16 [2, 2, 8, 1024, 576], P('section', None, 'shard', 'ctx')
- input_grads: bfloat16 [2, 2, 8, 1024, 576], P('section', None, 'shard', 'ctx')
- grad_attn_gain: float32 [2, 576], P('section', 'shard')
- grad_query: float32 [2, 576, 576], P('section', 'shard')
- grad_key: float32 [2, 576, 192], P('section', 'shard')
- grad_value: float32 [2, 576, 192], P('section', 'shard')
- grad_out: float32 [2, 576, 576], P('section', 'shard')
- grad_mlp_gain: float32 [2, 576], P('section', 'shard')
- grad_gate: float32 [2, 576, 1536], P('section', 'shard')
- grad_up: float32 [2, 576, 1536], P('section', 'shard')
- grad_down: float32 [2, 1536, 576], P('section', 'shard')
The draws below stay inside these ranges and needn't reach their ends.
All inputs are finite; a program needn't handle non-finite values.
Results may differ from the reference program's by a relative error of at most 0.025.
Values may be sent and summed in bfloat16 or wider, within the bound.
A program may use at most 256 MiB of HBM per device.

```python
import jax
import jax.numpy as jnp
from jax import lax

D = 576
HEADS = 9
KV_HEADS = 3
HEAD_DIM = 64
FF = 1536
SEQ_LEN = 1024
MICRO = 2
SECTIONS = 2
SEQS = 8
N_SECTION = 2


def block_levels(key, shape, pieces, smallest, largest):
    loudness = 1.0
    for axis_at, shards_of in pieces:
        heights = jax.random.uniform(jax.random.fold_in(jax.random.fold_in(key, 6), axis_at), (shards_of,), jnp.float32, smallest / len(pieces), largest / len(pieces))
        loudness = loudness * jnp.repeat(jnp.exp(heights), shape[axis_at] // shards_of).reshape((-1,) + (1,) * (len(shape) - 1 - axis_at))
    return loudness


def noise(rng, extent, width, most, split=(), held_as=jnp.bfloat16):
    loudness = block_levels(rng, extent, split, -0.22, 0.18) if split else 1.0
    result = jax.random.normal(rng, extent, jnp.float32) * width * loudness
    return jnp.minimum(jnp.maximum(result, -most), most).astype(held_as)


def setup_inputs(seed: int = 0) -> dict:
    seeds = jax.random.split(jax.random.key(seed), 12)
    inputs = noise(seeds[0], (MICRO, SEQS, SEQ_LEN, D), 1.0, 6.0, ((1, 8), (2, 2)))
    cotangent = noise(seeds[1], (MICRO, SEQS, SEQ_LEN, D), 1.0, 6.0, ((1, 8), (2, 2)))
    attn_gain = jnp.clip(1.0 + 0.1 * jax.random.normal(seeds[2], (SECTIONS, D), jnp.float32), 0.5, 1.5).astype(jnp.bfloat16)
    w_query = noise(seeds[3], (SECTIONS, D, HEADS * HEAD_DIM), D ** -0.5, 0.25, ((0, 2), (1, 8)))
    w_key = noise(seeds[4], (SECTIONS, D, KV_HEADS * HEAD_DIM), D ** -0.5, 0.25, ((0, 2), (1, 8)))
    w_value = noise(seeds[5], (SECTIONS, D, KV_HEADS * HEAD_DIM), D ** -0.5, 0.25, ((0, 2), (1, 8)))
    w_out = noise(seeds[6], (SECTIONS, HEADS * HEAD_DIM, D), (max(D // 128, 1)) ** -0.5, 3.0, ((0, 2), (1, 8)))
    mlp_gain = jnp.clip(1.0 + 0.1 * jax.random.normal(seeds[7], (SECTIONS, D), jnp.float32), 0.5, 1.5).astype(jnp.bfloat16)
    w_gate = noise(seeds[8], (SECTIONS, D, FF), D ** -0.5, 0.25, ((0, 2), (1, 8)))
    w_up = noise(seeds[9], (SECTIONS, D, FF), D ** -0.5, 0.25, ((0, 2), (1, 8)))
    w_down = noise(seeds[10], (SECTIONS, FF, D), FF ** -0.5, 0.15625, ((0, 2), (1, 8)))
    return {"inputs": inputs, "cotangent": cotangent, "attn_gain": attn_gain, "w_query": w_query, "w_key": w_key, "w_value": w_value, "w_out": w_out, "mlp_gain": mlp_gain, "w_gate": w_gate, "w_up": w_up, "w_down": w_down}


epsilon = 1e-05
rope_base = 100000.0
highest = lax.Precision.HIGHEST

@jax.custom_vjp
def low(v):
    return lax.optimization_barrier(v.astype(jnp.bfloat16)).astype(jnp.float32)

@jax.custom_vjp
def low_back(v):
    return v

def low_keep(v):
    return (low(v), None)

def low_pass(kept, grad):
    return (grad,)

def back_keep(v):
    return (v, None)

def back_low(kept, grad):
    return (low(grad),)
low.defvjp(low_keep, low_pass)
low_back.defvjp(back_keep, back_low)

def rope_tables(positions):
    half_dim = HEAD_DIM // 2
    frequency = rope_base ** (-(jnp.arange(half_dim).astype(jnp.float32) * 2.0 / HEAD_DIM))
    angles = positions.astype(jnp.float32)[:, None] * frequency[None, :]
    cosine = jnp.cos(angles)
    sine_table = jnp.sin(angles)
    return (jnp.concatenate([cosine, cosine], -1), jnp.concatenate([sine_table, sine_table], -1))

def rotate(source, cosine, sine_table):
    half_dim = source.shape[-1] // 2
    turned = jnp.concatenate([-source[..., half_dim:], source[..., :half_dim]], -1)
    return source * cosine[:, None, :] + turned * sine_table[:, None, :]

def rms_norm(source, gain_vec):
    return source * lax.rsqrt(lax.optimization_barrier(jnp.mean(source * source, -1, keepdims=True)) + epsilon) * gain_vec

def attend_one(queries, key_rows, values):
    scores = low_back(jnp.einsum('qkgd,jkd->kgqj', queries, key_rows, precision=highest) * HEAD_DIM ** (-0.5))
    causal = jnp.arange(SEQ_LEN)[None, :] <= jnp.arange(SEQ_LEN)[:, None]
    scores = jnp.where(causal, scores, -1e+30)
    row_max = lax.optimization_barrier(jnp.max(scores, -1, keepdims=True))
    exp_terms = jnp.exp(scores - row_max)
    attn_probs = low(exp_terms / lax.optimization_barrier(jnp.sum(exp_terms, -1, keepdims=True)))
    attn_mixed = jnp.einsum('kgqj,jkd->qkgd', attn_probs, values, precision=highest)
    return attn_mixed.reshape(SEQ_LEN, HEADS * HEAD_DIM)

def attend_triple(triple):
    return attend_one(triple[0], triple[1], triple[2])

def section_layer(hidden_in, weights):
    gain_attn, query_w, key_w, value_w, out_w, gain_mlp, gate_w, up_w, down_w = weights
    batch_size = hidden_in.shape[0]
    cosine, sine_table = rope_tables(jnp.arange(SEQ_LEN))
    normed = low(rms_norm(hidden_in, gain_attn))
    query_raw = low_back(jnp.dot(normed, query_w, precision=highest)).reshape(batch_size, SEQ_LEN, HEADS, HEAD_DIM)
    key_raw = low_back(jnp.dot(normed, key_w, precision=highest)).reshape(batch_size, SEQ_LEN, KV_HEADS, HEAD_DIM)
    queries = low(rotate(query_raw, cosine, sine_table)).reshape(batch_size, SEQ_LEN, KV_HEADS, HEADS // KV_HEADS, HEAD_DIM)
    key_rows = low(rotate(key_raw, cosine, sine_table))
    values = low_back(low(jnp.dot(normed, value_w, precision=highest))).reshape(batch_size, SEQ_LEN, KV_HEADS, HEAD_DIM)
    attn_mixed = lax.map(jax.checkpoint(attend_triple), (queries, key_rows, values))
    attn_mixed = low_back(low(attn_mixed))
    residual = hidden_in + low_back(jnp.dot(attn_mixed, out_w, precision=highest))
    normed_mlp = low(rms_norm(residual, gain_mlp))
    gate_pre = low_back(jnp.dot(normed_mlp, gate_w, precision=highest))
    up_proj = low_back(jnp.dot(normed_mlp, up_w, precision=highest))
    hidden = low(gate_pre * jax.nn.sigmoid(gate_pre) * up_proj)
    return residual + low_back(jnp.dot(hidden, down_w, precision=highest))

def forward(inputs_f, zeros_f, params):
    hidden_now = inputs_f
    sent_list = []
    for layer_pos in range(N_SECTION):
        if layer_pos > 0:
            hidden_now = low_back(hidden_now + zeros_f[layer_pos - 1])
        hidden_now = section_layer(hidden_now, tuple((tensor[layer_pos] for tensor in params)))
        if layer_pos + 1 < N_SECTION:
            hidden_now = low(hidden_now)
        sent_list.append(hidden_now)
    return (hidden_now, jnp.stack(sent_list))

def reference(inputs, cotangent, attn_gain, w_query, w_key, w_value, w_out, mlp_gain, w_gate, w_up, w_down):
    params = tuple((tensor.astype(jnp.float32) for tensor in (attn_gain, w_query, w_key, w_value, w_out, mlp_gain, w_gate, w_up, w_down)))
    batch_size = MICRO * SEQS
    inputs_f = inputs.astype(jnp.float32).reshape(batch_size, SEQ_LEN, D)
    zeros_f = jnp.zeros((N_SECTION - 1, batch_size, SEQ_LEN, D), jnp.float32)
    final_out, pullback, sent_all = jax.vjp(forward, inputs_f, zeros_f, params, has_aux=True)
    grad_in, grad_zero, grads_all = pullback(cotangent.astype(jnp.float32).reshape(batch_size, SEQ_LEN, D))
    full_shape = (N_SECTION, MICRO, SEQS, SEQ_LEN, D)
    activations = sent_all.reshape(full_shape).astype(jnp.bfloat16)
    input_grads = jnp.concatenate([grad_in[None], grad_zero], 0).reshape(full_shape).astype(jnp.bfloat16)
    return (activations, input_grads, grads_all[0], grads_all[1], grads_all[2], grads_all[3], grads_all[4], grads_all[5], grads_all[6], grads_all[7], grads_all[8])
```

```python
import functools

import jax
import jax.numpy as jnp
from jax import lax
from jax.experimental import pallas as pl
from jax.experimental.pallas import tpu as pltpu
from jax.sharding import PartitionSpec as P

HEADS = 9
KV_HEADS = 3
HEAD_DIM = 64
GROUPS = HEADS // KV_HEADS

epsilon = 1e-05
rope_base = 100000.0
f32 = jnp.float32
bf16 = jnp.bfloat16


def rope_tables(positions):
    half_dim = HEAD_DIM // 2
    frequency = rope_base ** (-(jnp.arange(half_dim).astype(f32) * 2.0 / HEAD_DIM))
    angles = frequency[:, None] * positions.astype(f32)[None, :]
    return jnp.cos(angles), jnp.sin(angles)


def rotate(source, cosine, sine):
    rows = source.shape[-1]
    pairs = source.reshape(-1, 2, HEAD_DIM // 2, rows)
    first, second = pairs[:, 0], pairs[:, 1]
    turned = jnp.stack(
        [first * cosine - second * sine, second * cosine + first * sine], axis=1
    )
    return turned.reshape(source.shape)


def inverse_rms(source):
    return lax.rsqrt(jnp.mean(source * source, -1, keepdims=True) + epsilon)


def norm_back(source, gain_vec, grad_normed, grad_carry):
    factor = inverse_rms(source)
    unit_rows = source * factor
    gain_grad = jnp.sum(grad_normed * unit_rows, axis=0)
    scaled = grad_normed * gain_vec
    back = factor * (scaled - unit_rows * jnp.mean(scaled * unit_rows, -1, keepdims=True))
    return grad_carry + back, gain_grad


def dot(left, right, left_dim, right_dim):
    return lax.dot_general(
        left, right, (((left_dim,), (right_dim,)), ((), ())), preferred_element_type=f32
    )


def visible(keys, rows):
    return lax.broadcasted_iota(jnp.int32, (keys, rows), 0) <= lax.broadcasted_iota(
        jnp.int32, (keys, rows), 1
    )


def attend_kernel(blocks, pos_ref, q_ref, kv_ref, mixed_ref, log_ref, acc_ref):
    rows = q_ref.shape[-1]
    here = pos_ref[0]
    width = KV_HEADS * HEAD_DIM
    shown = visible(rows, rows)

    def one_kv(kv):
        row0 = pl.multiple_of(kv * HEAD_DIM, HEAD_DIM)
        for g in range(GROUPS):
            q0 = pl.multiple_of((kv * GROUPS + g) * HEAD_DIM, HEAD_DIM)
            q = q_ref[pl.ds(q0, HEAD_DIM), :]

            def scores_at(c):
                k = kv_ref[c, pl.ds(row0, HEAD_DIM), :]
                return dot(k, q, 0, 0)

            s = jnp.where(shown, scores_at(here), -1e30)
            top = jnp.max(s, axis=0, keepdims=True)
            e = jnp.exp(s - top)
            total = jnp.sum(e, axis=0, keepdims=True)
            v = kv_ref[here, pl.ds(width + row0, HEAD_DIM), :]
            acc_ref[...] = dot(v, e.astype(bf16), 1, 0)

            def earlier(c, carry):
                top, total = carry
                s = scores_at(c)
                new_top = jnp.maximum(top, jnp.max(s, axis=0, keepdims=True))
                fade = jnp.exp(top - new_top)
                e = jnp.exp(s - new_top)
                v = kv_ref[c, pl.ds(width + row0, HEAD_DIM), :]
                acc_ref[...] = acc_ref[...] * fade + dot(v, e.astype(bf16), 1, 0)
                return new_top, total * fade + jnp.sum(e, axis=0, keepdims=True)

            top, total = lax.fori_loop(0, here, earlier, (top, total))
            mixed_ref[pl.ds(q0, HEAD_DIM), :] = (acc_ref[...] / total).astype(bf16)
            log_ref[pl.ds(kv * GROUPS + g, 1), :] = top + jnp.log(total)

    pl.loop(0, KV_HEADS)(one_kv)


def attend(pos, q, kv):
    blocks, _, rows = kv.shape
    vmem = pl.BlockSpec(memory_space=pltpu.VMEM)
    pairs = HEADS * rows * rows * blocks
    return pl.pallas_call(
        functools.partial(attend_kernel, blocks),
        out_shape=(
            jax.ShapeDtypeStruct(q.shape, bf16),
            jax.ShapeDtypeStruct((16, rows), f32),
        ),
        in_specs=[pl.BlockSpec(memory_space=pltpu.SMEM), vmem, vmem],
        out_specs=(vmem, vmem),
        scratch_shapes=[pltpu.VMEM((HEAD_DIM, rows), f32)],
        compiler_params=pltpu.CompilerParams(vmem_limit_bytes=40 * 2**20),
        cost_estimate=pl.CostEstimate(
            flops=16 * pairs * HEAD_DIM, bytes_accessed=4 * 2**20, transcendentals=pairs
        ),
    )(pos, q, kv)


def attend_back_kernel(blocks, pos_ref, q_ref, kv_ref, log_ref, dm_ref, dq_ref, dkv_ref,
                       keep_p, keep_d, acc_ref):
    rows = q_ref.shape[-1]
    here = pos_ref[0]
    width = KV_HEADS * HEAD_DIM
    shown = visible(rows, rows)
    dkv_ref[...] = jnp.zeros_like(dkv_ref)

    def one_kv(kv):
        row0 = pl.multiple_of(kv * HEAD_DIM, HEAD_DIM)
        for g in range(GROUPS):
            q0 = pl.multiple_of((kv * GROUPS + g) * HEAD_DIM, HEAD_DIM)
            q = q_ref[pl.ds(q0, HEAD_DIM), :]
            dm = dm_ref[pl.ds(q0, HEAD_DIM), :]
            log_total = log_ref[pl.ds(kv * GROUPS + g, 1), :]

            def first_pass(c, masked):
                k = kv_ref[c, pl.ds(row0, HEAD_DIM), :]
                v = kv_ref[c, pl.ds(width + row0, HEAD_DIM), :]
                p = jnp.exp(dot(k, q, 0, 0) - log_total)
                if masked:
                    p = jnp.where(shown, p, 0.0)
                d = dot(v, dm, 0, 0)
                keep_p[c] = p
                keep_d[c] = d
                return jnp.sum(p * d, axis=0, keepdims=True)

            delta = first_pass(here, True)
            delta = lax.fori_loop(0, here, lambda c, t: t + first_pass(c, False), delta)
            acc_ref[...] = jnp.zeros_like(acc_ref)

            def second_pass(c, _):
                p = keep_p[c]
                ds = (p * (keep_d[c] - delta)).astype(bf16)
                k = kv_ref[c, pl.ds(row0, HEAD_DIM), :]
                acc_ref[...] += dot(k, ds, 1, 0)
                dkv_ref[c, pl.ds(row0, HEAD_DIM), :] += dot(q, ds, 1, 1)
                dkv_ref[c, pl.ds(width + row0, HEAD_DIM), :] += dot(dm, p.astype(bf16), 1, 1)
                return 0

            lax.fori_loop(0, here + 1, second_pass, 0)
            dq_ref[pl.ds(q0, HEAD_DIM), :] = acc_ref[...]

    pl.loop(0, KV_HEADS)(one_kv)


def attend_back(pos, q, kv, log_total, dm):
    blocks, _, rows = kv.shape
    vmem = pl.BlockSpec(memory_space=pltpu.VMEM)
    pairs = HEADS * rows * rows * blocks
    return pl.pallas_call(
        functools.partial(attend_back_kernel, blocks),
        out_shape=(
            jax.ShapeDtypeStruct(q.shape, f32),
            jax.ShapeDtypeStruct(kv.shape, f32),
        ),
        in_specs=[pl.BlockSpec(memory_space=pltpu.SMEM)] + [vmem] * 4,
        out_specs=(vmem, vmem),
        scratch_shapes=[
            pltpu.VMEM((blocks, rows, rows), f32),
            pltpu.VMEM((blocks, rows, rows), f32),
            pltpu.VMEM((HEAD_DIM, rows), f32),
        ],
        compiler_params=pltpu.CompilerParams(vmem_limit_bytes=40 * 2**20),
        cost_estimate=pl.CostEstimate(
            flops=40 * pairs * HEAD_DIM, bytes_accessed=8 * 2**20, transcendentals=pairs
        ),
    )(pos, q, kv, log_total, dm)


def exchange(x, axis, bit=1):
    return lax.ppermute(x, axis, [(i, i ^ bit) for i in range(lax.axis_size(axis))])


def gathered(piece):
    return lax.all_gather(piece, "shard", axis=0, tiled=True)


def reduce_rows(grad):
    devices = lax.axis_size("shard")
    me = lax.axis_index("shard")
    part = grad.astype(bf16).reshape(devices, -1, grad.shape[-1])
    bit = 1
    while bit < devices:
        mine = (me // bit) % 2
        halves = part.reshape(part.shape[0] // 2, 2, *part.shape[1:])
        keep = lax.dynamic_index_in_dim(halves, mine, 1, keepdims=False)
        send = lax.dynamic_index_in_dim(halves, 1 - mine, 1, keepdims=False)
        part = (keep.astype(f32) + exchange(send, "shard", bit).astype(f32)).astype(bf16)
        bit *= 2
    return part[0]


def sum_ctx(part):
    if lax.axis_size("ctx") == 2:
        return part.astype(f32) + exchange(part, "ctx").astype(f32)
    return lax.psum(part, "ctx").astype(f32)


def forward_layer(layer_in, weights, pos, cosine, sine):
    gain_attn, gain_mlp, qkv_w, out_w, gate_up_w, down_w = weights
    hidden_in = layer_in.astype(f32)
    normed = (hidden_in * inverse_rms(hidden_in) * gain_attn).astype(bf16)
    raw = dot(qkv_w, normed, 0, 1)
    q_width = HEADS * HEAD_DIM
    kv_width = KV_HEADS * HEAD_DIM
    queries = (rotate(raw[:q_width], cosine, sine).astype(bf16) * HEAD_DIM**-0.5).astype(bf16)
    keys = rotate(raw[q_width : q_width + kv_width], cosine, sine).astype(bf16)
    values = raw[q_width + kv_width :].astype(bf16)
    kv = lax.all_gather(jnp.concatenate([keys, values], 0), "ctx", axis=0)
    mixed, log_total = attend(pos, queries, kv)
    residual = hidden_in + dot(mixed, out_w, 0, 0)
    normed_mlp = (residual * inverse_rms(residual) * gain_mlp).astype(bf16)
    gate_up = dot(normed_mlp, gate_up_w, 1, 0)
    ff = gate_up.shape[-1] // 2
    gate, up = gate_up[:, :ff], gate_up[:, ff:]
    hidden = (gate * jax.nn.sigmoid(gate) * up).astype(bf16)
    layer_out = (residual + dot(hidden, down_w, 1, 0)).astype(bf16)
    stored = (layer_in, normed, queries, kv, log_total, mixed, residual, normed_mlp, gate_up, hidden)
    return layer_out, stored


def backward_layer(grad_out, stored, weights, pos, cosine, sine):
    gain_attn, gain_mlp, qkv_w, out_w, gate_up_w, down_w = weights
    layer_in, normed, queries, kv, log_total, mixed, residual, normed_mlp, gate_up, hidden = stored
    ff = gate_up.shape[-1] // 2
    gate, up = gate_up[:, :ff], gate_up[:, ff:]
    g_down = dot(hidden, grad_out, 0, 0)
    d_hidden = dot(grad_out, down_w, 1, 1)
    sig = jax.nn.sigmoid(gate)
    d_gate = (d_hidden * up * sig * (1.0 + gate * (1.0 - sig))).astype(bf16)
    d_up = (d_hidden * gate * sig).astype(bf16)
    d_gate_up = jnp.concatenate([d_gate, d_up], 1)
    g_gate_up = dot(normed_mlp, d_gate_up, 0, 0)
    d_normed = dot(d_gate_up, gate_up_w, 1, 1)
    d_res, g_gain_mlp = norm_back(residual, gain_mlp, d_normed, grad_out.astype(f32))
    d_attn = d_res.astype(bf16)
    g_out = dot(mixed, d_attn, 1, 0)
    d_mixed = dot(out_w, d_attn, 1, 1).astype(bf16)
    d_queries, d_kv = attend_back(pos, queries, kv, log_total, d_mixed)
    d_kv = d_kv.astype(bf16)
    if lax.axis_size("ctx") == 2:
        me = lax.axis_index("ctx")
        own = lax.dynamic_index_in_dim(d_kv, me, 0, keepdims=False).astype(f32)
        other = lax.dynamic_index_in_dim(d_kv, 1 - me, 0, keepdims=False)
        d_kv = own + exchange(other, "ctx").astype(f32)
    else:
        d_kv = lax.psum_scatter(d_kv, "ctx", scatter_dimension=0).astype(f32)
    kv_width = KV_HEADS * HEAD_DIM
    d_q = rotate(d_queries * HEAD_DIM**-0.5, cosine, -sine).astype(bf16)
    d_k = rotate(d_kv[:kv_width], cosine, -sine).astype(bf16)
    d_v = d_kv[kv_width:].astype(bf16)
    d_qkv = jnp.concatenate([d_q, d_k, d_v], 0)
    g_qkv = dot(normed, d_qkv, 0, 1)
    d_n = dot(d_qkv, qkv_w, 0, 1)
    grad_in, g_gain_attn = norm_back(layer_in.astype(f32), gain_attn, d_n, d_res)
    gains = jnp.stack([g_gain_attn, g_gain_mlp], 1)
    late = jnp.concatenate([g_qkv, gains], 1)
    return grad_in.astype(bf16), (g_down, g_gate_up, g_out, late)


def local(
    inputs, cotangent, attn_gain, w_query, w_key, w_value, w_out, mlp_gain, w_gate, w_up, w_down
):
    layers = lax.axis_size("section")
    section = lax.axis_index("section")
    block_pos = lax.axis_index("ctx")
    _, _, rows, width = inputs.shape
    pos = jnp.reshape(block_pos, (1,)).astype(jnp.int32)
    cosine, sine = rope_tables(block_pos * rows + jnp.arange(rows))
    qkv_cols = w_query.shape[-1] + w_key.shape[-1] + w_value.shape[-1]

    early = jnp.concatenate(
        [w_query[0], w_key[0], w_value[0], attn_gain[0][:, None], mlp_gain[0][:, None]], 1
    )
    pieces = (early, w_out[0], jnp.concatenate([w_gate[0], w_up[0]], 1), w_down[0])

    def both(piece):
        other = exchange(piece, "section")
        return [jnp.where(section == l, piece, other) for l in range(layers)]

    shards = [both(piece) for piece in pieces]
    weights = []
    for l in range(layers):
        early_all, out_all, gate_up_all, down_all = [gathered(s[l]) for s in shards]
        gains = early_all[:, qkv_cols:].astype(f32).T
        weights.append(
            (gains[0:1], gains[1:2], early_all[:, :qkv_cols], out_all, gate_up_all, down_all)
        )

    hidden_now = lax.dynamic_index_in_dim(inputs, section, 0, keepdims=False)[0]
    outs, kept = [], []
    for l in range(layers):
        hidden_now, stored = forward_layer(hidden_now, weights[l], pos, cosine, sine)
        outs.append(hidden_now)
        kept.append(stored)

    grad = lax.dynamic_index_in_dim(cotangent, section, 0, keepdims=False)[0]
    in_grads, parts = [None] * layers, [None] * layers
    for l in reversed(range(layers)):
        grad, raw = backward_layer(grad, kept[l], weights[l], pos, cosine, sine)
        in_grads[l] = grad
        parts[l] = [reduce_rows(g) for g in raw]

    def swap(per_layer):
        mine = jnp.where(section == 0, per_layer[0], per_layer[1])
        other = exchange(jnp.where(section == 0, per_layer[1], per_layer[0]), "section")
        return mine, other

    def both_micro(per_layer):
        mine, other = swap(per_layer)
        first = jnp.where(section == 0, mine, other)
        second = jnp.where(section == 0, other, mine)
        return jnp.stack([first, second])[None, :, None]

    finals = []
    for pair in zip(*parts):
        mine, other = swap(pair)
        finals.append(sum_ctx((mine.astype(f32) + other.astype(f32)).astype(bf16)))
    g_down, g_gate_up, g_out, late = finals
    ff = w_gate.shape[-1]
    a, b = w_query.shape[-1], w_query.shape[-1] + w_key.shape[-1]
    return (
        both_micro(outs),
        both_micro(in_grads),
        late[None, :, qkv_cols],
        late[None, :, :a],
        late[None, :, a:b],
        late[None, :, b:qkv_cols],
        g_out[None],
        late[None, :, qkv_cols + 1],
        g_gate_up[None, :, :ff],
        g_gate_up[None, :, ff:],
        g_down[None],
    )


def solution(mesh):
    tokens = P(None, "shard", "ctx", None)
    gain = P("section", "shard")
    matrix = P("section", "shard", None)
    result = P("section", None, "shard", "ctx", None)
    return jax.shard_map(
        local,
        mesh=mesh,
        in_specs=(tokens, tokens, gain, matrix, matrix, matrix, matrix, gain, matrix, matrix, matrix),
        out_specs=(result, result, gain, matrix, matrix, matrix, matrix, gain, matrix, matrix, matrix),
        check_vma=False,
    )
```

```python
import functools

import jax
import jax.numpy as jnp
from jax import lax
from jax.experimental import pallas as pl
from jax.experimental.pallas import tpu as pltpu
from jax.sharding import PartitionSpec as P

HEADS = 9
KV_HEADS = 3
HEAD_DIM = 64
GROUPS = HEADS // KV_HEADS
PAD = 256

epsilon = 1e-05
rope_base = 100000.0
f32 = jnp.float32
bf16 = jnp.bfloat16


def rope_tables(positions):
    half_dim = HEAD_DIM // 2
    frequency = rope_base ** (-(jnp.arange(half_dim).astype(f32) * 2.0 / HEAD_DIM))
    angles = frequency[:, None] * positions.astype(f32)[None, :]
    return jnp.cos(angles), jnp.sin(angles)


def rotate(source, cosine, sine):
    rows = source.shape[-1]
    pairs = source.reshape(-1, 2, HEAD_DIM // 2, rows)
    first, second = pairs[:, 0], pairs[:, 1]
    turned = jnp.stack(
        [first * cosine - second * sine, second * cosine + first * sine], axis=1
    )
    return turned.reshape(source.shape)


def inverse_rms(source):
    return lax.rsqrt(jnp.mean(source * source, -1, keepdims=True) + epsilon)


def norm_back(source, gain_vec, grad_normed, grad_carry):
    factor = inverse_rms(source)
    unit_rows = source * factor
    gain_grad = jnp.sum(grad_normed * unit_rows, axis=0)
    scaled = grad_normed * gain_vec
    back = factor * (scaled - unit_rows * jnp.mean(scaled * unit_rows, -1, keepdims=True))
    return grad_carry + back, gain_grad


def dot(left, right, left_dim, right_dim):
    return lax.dot_general(
        left, right, (((left_dim,), (right_dim,)), ((), ())), preferred_element_type=f32
    )


def visible(keys, rows):
    return lax.broadcasted_iota(jnp.int32, (keys, rows), 0) <= lax.broadcasted_iota(
        jnp.int32, (keys, rows), 1
    )


def attend_kernel(blocks, pos_ref, q_ref, kv_ref, mixed_ref, log_ref, acc_ref):
    rows = q_ref.shape[-1]
    here = pos_ref[0]
    width = KV_HEADS * HEAD_DIM
    shown = visible(rows, rows)

    def one_kv(kv):
        row0 = pl.multiple_of(kv * HEAD_DIM, HEAD_DIM)
        for g in range(GROUPS):
            q0 = pl.multiple_of((kv * GROUPS + g) * HEAD_DIM, HEAD_DIM)
            q = q_ref[pl.ds(q0, HEAD_DIM), :]

            def scores_at(c):
                k = kv_ref[c, pl.ds(row0, HEAD_DIM), :]
                return dot(k, q, 0, 0)

            s = jnp.where(shown, scores_at(here), -1e30)
            top = jnp.max(s, axis=0, keepdims=True)
            e = jnp.exp(s - top)
            total = jnp.sum(e, axis=0, keepdims=True)
            v = kv_ref[here, pl.ds(width + row0, HEAD_DIM), :]
            acc_ref[...] = dot(v, e.astype(bf16), 1, 0)

            def earlier(c, carry):
                top, total = carry
                s = scores_at(c)
                new_top = jnp.maximum(top, jnp.max(s, axis=0, keepdims=True))
                fade = jnp.exp(top - new_top)
                e = jnp.exp(s - new_top)
                v = kv_ref[c, pl.ds(width + row0, HEAD_DIM), :]
                acc_ref[...] = acc_ref[...] * fade + dot(v, e.astype(bf16), 1, 0)
                return new_top, total * fade + jnp.sum(e, axis=0, keepdims=True)

            top, total = lax.fori_loop(0, here, earlier, (top, total))
            mixed_ref[pl.ds(q0, HEAD_DIM), :] = (acc_ref[...] / total).astype(bf16)
            log_ref[pl.ds(kv * GROUPS + g, 1), :] = top + jnp.log(total)

    pl.loop(0, KV_HEADS)(one_kv)


def attend(pos, q, kv):
    blocks, _, rows = kv.shape
    vmem = pl.BlockSpec(memory_space=pltpu.VMEM)
    pairs = HEADS * rows * rows * blocks
    return pl.pallas_call(
        functools.partial(attend_kernel, blocks),
        out_shape=(
            jax.ShapeDtypeStruct(q.shape, bf16),
            jax.ShapeDtypeStruct((16, rows), f32),
        ),
        in_specs=[pl.BlockSpec(memory_space=pltpu.SMEM), vmem, vmem],
        out_specs=(vmem, vmem),
        scratch_shapes=[pltpu.VMEM((HEAD_DIM, rows), f32)],
        compiler_params=pltpu.CompilerParams(vmem_limit_bytes=40 * 2**20),
        cost_estimate=pl.CostEstimate(
            flops=16 * pairs * HEAD_DIM, bytes_accessed=4 * 2**20, transcendentals=pairs
        ),
    )(pos, q, kv)


def attend_back_kernel(blocks, pos_ref, q_ref, kv_ref, log_ref, dm_ref, dq_ref, dkv_ref,
                       keep_p, keep_d, acc_ref):
    rows = q_ref.shape[-1]
    here = pos_ref[0]
    width = KV_HEADS * HEAD_DIM
    shown = visible(rows, rows)
    dkv_ref[...] = jnp.zeros_like(dkv_ref)

    def one_kv(kv):
        row0 = pl.multiple_of(kv * HEAD_DIM, HEAD_DIM)
        for g in range(GROUPS):
            q0 = pl.multiple_of((kv * GROUPS + g) * HEAD_DIM, HEAD_DIM)
            q = q_ref[pl.ds(q0, HEAD_DIM), :]
            dm = dm_ref[pl.ds(q0, HEAD_DIM), :]
            log_total = log_ref[pl.ds(kv * GROUPS + g, 1), :]

            def first_pass(c, masked):
                k = kv_ref[c, pl.ds(row0, HEAD_DIM), :]
                v = kv_ref[c, pl.ds(width + row0, HEAD_DIM), :]
                p = jnp.exp(dot(k, q, 0, 0) - log_total)
                if masked:
                    p = jnp.where(shown, p, 0.0)
                d = dot(v, dm, 0, 0)
                keep_p[c] = p
                keep_d[c] = d
                return jnp.sum(p * d, axis=0, keepdims=True)

            delta = first_pass(here, True)
            delta = lax.fori_loop(0, here, lambda c, t: t + first_pass(c, False), delta)
            acc_ref[...] = jnp.zeros_like(acc_ref)

            def second_pass(c, _):
                p = keep_p[c]
                ds = (p * (keep_d[c] - delta)).astype(bf16)
                k = kv_ref[c, pl.ds(row0, HEAD_DIM), :]
                acc_ref[...] += dot(k, ds, 1, 0)
                dkv_ref[c, pl.ds(row0, HEAD_DIM), :] += dot(q, ds, 1, 1)
                dkv_ref[c, pl.ds(width + row0, HEAD_DIM), :] += dot(dm, p.astype(bf16), 1, 1)
                return 0

            lax.fori_loop(0, here + 1, second_pass, 0)
            dq_ref[pl.ds(q0, HEAD_DIM), :] = acc_ref[...]

    pl.loop(0, KV_HEADS)(one_kv)


def attend_back(pos, q, kv, log_total, dm):
    blocks, _, rows = kv.shape
    vmem = pl.BlockSpec(memory_space=pltpu.VMEM)
    pairs = HEADS * rows * rows * blocks
    return pl.pallas_call(
        functools.partial(attend_back_kernel, blocks),
        out_shape=(
            jax.ShapeDtypeStruct(q.shape, f32),
            jax.ShapeDtypeStruct(kv.shape, f32),
        ),
        in_specs=[pl.BlockSpec(memory_space=pltpu.SMEM)] + [vmem] * 4,
        out_specs=(vmem, vmem),
        scratch_shapes=[
            pltpu.VMEM((blocks, rows, rows), f32),
            pltpu.VMEM((blocks, rows, rows), f32),
            pltpu.VMEM((HEAD_DIM, rows), f32),
        ],
        compiler_params=pltpu.CompilerParams(vmem_limit_bytes=40 * 2**20),
        cost_estimate=pl.CostEstimate(
            flops=40 * pairs * HEAD_DIM, bytes_accessed=8 * 2**20, transcendentals=pairs
        ),
    )(pos, q, kv, log_total, dm)


def exchange(x, axis, bit=1):
    return lax.ppermute(x, axis, [(i, i ^ bit) for i in range(lax.axis_size(axis))])


def pair_up(mine, own, other, axis):
    low = jnp.where(mine == 0, own, other)
    high = jnp.where(mine == 0, other, own)
    return jnp.concatenate([low, high], axis)


def tie(*values):
    return lax.optimization_barrier(values)


class Gathering:
    def __init__(self, piece, split):
        self.split = split
        self.part = piece[None]
        self.halved = lax.axis_size("ctx") == 2
        if self.halved:
            half = self.part.shape[split] // 2
            self.part = lax.dynamic_slice_in_dim(
                self.part, lax.axis_index("ctx") * half, half, split
            )
        self.todo = []
        bit = lax.axis_size("shard") // 2
        while bit > 1:
            self.todo.append(bit)
            bit //= 2
        self.todo += (["ctx"] if self.halved else []) + ["core"]

    def step(self):
        what = self.todo.pop(0)
        me = lax.axis_index("shard")
        held = self.part
        if what == "ctx":
            self.part = pair_up(lax.axis_index("ctx"), held, exchange(held, "ctx"), self.split)
        else:
            bit = 1 if what == "core" else what
            other = exchange(held, "shard", bit)
            joined = pair_up((me // bit) % 2, held[:, None], other[:, None], 1)
            self.part = joined.reshape(-1, *held.shape[1:])

    def finish(self):
        while self.todo:
            self.step()
        return self.part.reshape(-1, self.part.shape[-1])


class Reduction:
    def __init__(self, grad, split):
        devices = lax.axis_size("shard")
        self.split = split
        self.part = grad.astype(bf16).reshape(devices, -1, grad.shape[-1])
        self.halved = lax.axis_size("ctx") == 2
        self.todo = []
        bit = 1
        while bit < devices:
            self.todo.append(bit)
            bit *= 2
        if self.halved:
            self.todo.insert(2, "ctx")

    def step(self):
        if not self.todo:
            return
        what = self.todo.pop(0)
        part = self.part
        if what == "ctx":
            mine = lax.axis_index("ctx")
            half = part.shape[self.split] // 2
            keep = lax.dynamic_slice_in_dim(part, mine * half, half, self.split)
            send = lax.dynamic_slice_in_dim(part, (1 - mine) * half, half, self.split)
            got = exchange(send, "ctx")
        else:
            mine = (lax.axis_index("shard") // what) % 2
            halves = part.reshape(part.shape[0] // 2, 2, *part.shape[1:])
            keep = lax.dynamic_index_in_dim(halves, mine, 1, keepdims=False)
            send = lax.dynamic_index_in_dim(halves, 1 - mine, 1, keepdims=False)
            got = exchange(send, "shard", what)
        self.part = (keep.astype(f32) + got.astype(f32)).astype(bf16)

    def finish(self):
        while self.todo:
            self.step()
        return self.part

    def whole(self, part):
        if self.halved:
            return pair_up(lax.axis_index("ctx"), part, exchange(part, "ctx"), self.split)[0].astype(f32)
        return lax.psum(part, "ctx")[0].astype(f32)


def advance(value, reductions):
    reductions = [r for r in reductions if r.todo]
    if not reductions:
        return value
    for r in reductions:
        r.step()
    tied = lax.optimization_barrier((value, *[r.part for r in reductions]))
    for r, part in zip(reductions, tied[1:]):
        r.part = part
    return tied[0]


def forward_layer(layer_in, gathers, later, cols, pos, cosine, sine):
    early, gate_up_g, down_g = gathers
    qkv_cols, attn_cols = cols
    early_w = early.finish()
    gains = early_w[:, attn_cols : attn_cols + 2].astype(f32).T
    gain_attn, gain_mlp = gains[0:1], gains[1:2]
    qkv_w, out_w = early_w[:, :qkv_cols], early_w[:, qkv_cols:attn_cols]
    hidden_in = layer_in.astype(f32)
    normed = (hidden_in * inverse_rms(hidden_in) * gain_attn).astype(bf16)
    raw = dot(qkv_w, normed, 0, 1)
    q_width = HEADS * HEAD_DIM
    kv_width = KV_HEADS * HEAD_DIM
    queries = (rotate(raw[:q_width], cosine, sine).astype(bf16) * HEAD_DIM**-0.5).astype(bf16)
    keys = rotate(raw[q_width : q_width + kv_width], cosine, sine).astype(bf16)
    values = raw[q_width + kv_width :].astype(bf16)
    kv = jnp.concatenate([keys, values], 0)
    if lax.axis_size("ctx") == 2:
        kv = pair_up(lax.axis_index("ctx"), kv[None], exchange(kv, "ctx")[None], 0)
    else:
        kv = lax.all_gather(kv, "ctx", axis=0)
    mixed, log_total = attend(pos, queries, kv)
    residual = hidden_in + dot(mixed, out_w, 0, 0)
    normed_mlp = (residual * inverse_rms(residual) * gain_mlp).astype(bf16)
    gate_up_w, down_w = gate_up_g.finish(), down_g.finish()
    gate_up = dot(normed_mlp, gate_up_w, 1, 0)
    ff = gate_up.shape[-1] // 2
    gate, up = gate_up[:, :ff], gate_up[:, ff:]
    hidden = (gate * jax.nn.sigmoid(gate) * up).astype(bf16)
    layer_out = (residual + dot(hidden, down_w, 1, 0)).astype(bf16)
    weights = (gain_attn, gain_mlp, qkv_w, out_w, gate_up_w, down_w)
    stored = (layer_in, normed, queries, kv, log_total, mixed, residual, normed_mlp, gate_up, hidden)
    return layer_out, stored, weights


def backward_layer(grad_out, stored, weights, pos, cosine, sine, running):
    gain_attn, gain_mlp, qkv_w, out_w, gate_up_w, down_w = weights
    layer_in, normed, queries, kv, log_total, mixed, residual, normed_mlp, gate_up, hidden = stored
    ff = gate_up.shape[-1] // 2
    gate, up = gate_up[:, :ff], gate_up[:, ff:]
    g_down = dot(hidden, grad_out, 0, 0).astype(bf16)
    d_hidden = dot(grad_out, down_w, 1, 1)
    sig = jax.nn.sigmoid(gate)
    d_gate = (d_hidden * up * sig * (1.0 + gate * (1.0 - sig))).astype(bf16)
    d_up = (d_hidden * gate * sig).astype(bf16)
    d_gate_up = jnp.concatenate([d_gate, d_up], 1)
    g_gate_up = dot(normed_mlp, d_gate_up, 0, 0).astype(bf16)
    d_normed = dot(d_gate_up, gate_up_w, 1, 1)
    d_res, g_gain_mlp = norm_back(residual, gain_mlp, d_normed, grad_out.astype(f32))
    d_attn = d_res.astype(bf16)
    g_out = dot(mixed, d_attn, 1, 0)
    d_mixed = dot(out_w, d_attn, 1, 1).astype(bf16)
    d_mixed = advance(d_mixed, running)
    running = running + [Reduction(g_down, 1), Reduction(g_gate_up, 2)]
    d_queries, d_kv = attend_back(pos, queries, kv, log_total, d_mixed)
    d_kv = d_kv.astype(bf16)
    d_queries = advance(d_queries, running)
    if lax.axis_size("ctx") == 2:
        me = lax.axis_index("ctx")
        own = lax.dynamic_index_in_dim(d_kv, me, 0, keepdims=False).astype(f32)
        other = lax.dynamic_index_in_dim(d_kv, 1 - me, 0, keepdims=False)
        d_kv = own + exchange(other, "ctx").astype(f32)
    else:
        d_kv = lax.psum_scatter(d_kv, "ctx", scatter_dimension=0).astype(f32)
    kv_width = KV_HEADS * HEAD_DIM
    d_q = rotate(d_queries * HEAD_DIM**-0.5, cosine, -sine).astype(bf16)
    d_k = rotate(d_kv[:kv_width], cosine, -sine).astype(bf16)
    d_v = d_kv[kv_width:].astype(bf16)
    d_qkv = jnp.concatenate([d_q, d_k, d_v], 0)
    g_qkv = dot(normed, d_qkv, 0, 1)
    d_n = dot(d_qkv, qkv_w, 0, 1)
    grad_in, g_gain_attn = norm_back(layer_in.astype(f32), gain_attn, d_n, d_res)
    rest = jnp.zeros((g_out.shape[0], PAD - 2), f32)
    late = [g_qkv, g_out, g_gain_attn[:, None], g_gain_mlp[:, None], rest]
    late = jnp.concatenate([g.astype(bf16) for g in late], 1)
    running = running + [Reduction(late, 2)]
    return grad_in.astype(bf16), running


def local(
    inputs, cotangent, attn_gain, w_query, w_key, w_value, w_out, mlp_gain, w_gate, w_up, w_down
):
    layers = lax.axis_size("section")
    section = lax.axis_index("section")
    block_pos = lax.axis_index("ctx")
    _, _, rows, width = inputs.shape
    pos = jnp.reshape(block_pos, (1,)).astype(jnp.int32)
    cosine, sine = rope_tables(block_pos * rows + jnp.arange(rows))
    qkv_cols = w_query.shape[-1] + w_key.shape[-1] + w_value.shape[-1]

    attn_cols = qkv_cols + w_out.shape[-1]
    early = jnp.concatenate(
        [
            w_query[0], w_key[0], w_value[0], w_out[0],
            attn_gain[0][:, None], mlp_gain[0][:, None],
            jnp.zeros((w_out.shape[1], PAD - 2), bf16),
        ],
        1,
    )
    pieces = (early, jnp.concatenate([w_gate[0], w_up[0]], 1), w_down[0])

    others = [exchange(early, "section")]
    pieces = (early, *tie(others[0], *pieces[1:])[1:])
    others += [exchange(piece, "section") for piece in pieces[1:]]
    shards = [
        [jnp.where(section == l, piece, other) for l in range(layers)]
        for piece, other in zip(pieces, others)
    ]
    cols = (qkv_cols, attn_cols)
    gathers = []
    for l in range(layers):
        early_g = Gathering(shards[0][l], 2)
        if l == 0:
            early_g.todo = []
            early_g.part = lax.all_gather(shards[0][l], "shard", axis=0)
        gathers.append([early_g, Gathering(shards[1][l], 2), Gathering(shards[2][l], 1)])

    hidden_now = lax.dynamic_index_in_dim(inputs, section, 0, keepdims=False)[0]
    outs, kept, weights = [], [], []
    for l in range(layers):
        later = gathers[l + 1] if l + 1 < layers else []
        hidden_now, stored, weight = forward_layer(
            hidden_now, gathers[l], later, cols, pos, cosine, sine
        )
        weights.append(weight)
        outs.append(hidden_now)
        kept.append(stored)

    grad = lax.dynamic_index_in_dim(cotangent, section, 0, keepdims=False)[0]
    in_grads, running = [None] * layers, []
    for l in reversed(range(layers)):
        grad, running = backward_layer(grad, kept[l], weights[l], pos, cosine, sine, running)
        in_grads[l] = grad
    parts = [running[3 * i : 3 * i + 3] for i in reversed(range(layers))]

    def swap(per_layer):
        mine = jnp.where(section == 0, per_layer[0], per_layer[1])
        other = exchange(jnp.where(section == 0, per_layer[1], per_layer[0]), "section")
        return mine, other

    def both_micro(per_layer):
        mine, other = swap(per_layer)
        first = jnp.where(section == 0, mine, other)
        second = jnp.where(section == 0, other, mine)
        return jnp.stack([first, second])[None, :, None]

    finals = []
    for pair in zip(*parts):
        mine, other = swap([r.finish() for r in pair])
        total = (mine.astype(f32) + other.astype(f32)).astype(bf16)
        finals.append(pair[0].whole(total))
    g_down, g_gate_up, late = finals
    ff = w_gate.shape[-1]
    a, b = w_query.shape[-1], w_query.shape[-1] + w_key.shape[-1]
    return (
        both_micro(outs),
        both_micro(in_grads),
        late[None, :, attn_cols],
        late[None, :, :a],
        late[None, :, a:b],
        late[None, :, b:qkv_cols],
        late[None, :, qkv_cols:attn_cols],
        late[None, :, attn_cols + 1],
        g_gate_up[None, :, :ff],
        g_gate_up[None, :, ff:],
        g_down[None],
    )


def solution(mesh):
    tokens = P(None, "shard", "ctx", None)
    gain = P("section", "shard")
    matrix = P("section", "shard", None)
    result = P("section", None, "shard", "ctx", None)
    return jax.shard_map(
        local,
        mesh=mesh,
        in_specs=(tokens, tokens, gain, matrix, matrix, matrix, matrix, gain, matrix, matrix, matrix),
        out_specs=(result, result, gain, matrix, matrix, matrix, matrix, gain, matrix, matrix, matrix),
        check_vma=False,
    )
```
